1024 devices in a mesh: dp: 128 (over z, y_lo, x), peer: 8 (over y_hi, core).
Axes of the slice: x: 8, y: 8 (y_hi: 4, y_lo: 2; y = y_hi * 2 + y_lo), z: 8, core: 2. Of those that a mesh axis runs over, the one named last changes fastest.
Arguments:
- grads: bfloat16 [128, 2, 128, 8192], P('dp', None, 'peer'), may hold values from -0.796875 to 0.796875
- params: float32 [2, 8, 131072], P(None, 'peer', 'dp'), may hold values from -6 to 6
- moment1: float32 [2, 8, 131072], P(None, 'peer', 'dp'), may hold values from -2 to 2
- moment2: float32 [2, 8, 131072], P(None, 'peer', 'dp'), may hold values from 0.01 to 1
- base_params: float32 [2, 8, 131072], P(None, 'peer', 'dp'), may hold values from -6 to 6
- base_m1: float32 [2, 8, 131072], P(None, 'peer', 'dp'), may hold values from -2 to 2
- base_m2: float32 [2, 8, 131072], P(None, 'peer', 'dp'), may hold values from 0.01 to 1
- coef_num: int32 [4, 8], replicated, may hold values from -8 to 8, as said below
Outputs:
- new_params: float32 [2, 8, 131072], P(None, 'peer', 'dp')
- new_m1: float32 [2, 8, 131072], P(None, 'peer', 'dp')
- new_m2: float32 [2, 8, 131072], P(None, 'peer', 'dp')
- weights: bfloat16 [2, 128, 8192], P(None, 'peer')
- parity: float32 [4, 3, 2, 131072], P(None, None, None, ('dp', 'peer'))
The draws below stay inside these ranges and needn't reach their ends.
Inputs may be any that keep to these rules, and one draw needn't show every extreme that they name: `coef_num`: never zero.
All inputs are finite; a program needn't handle non-finite values.
Results may differ from the reference program's by a relative error of at most 0.001.
Values may be sent and summed in bfloat16 or wider, within the bound.
No kernel may reach another device: no remote copies, remote signals or barrier semaphores. Data moves between devices by JAX's collectives and lax.ppermute only.
A program may use at most 32 MiB of HBM per device.

```python
import math
import jax
import jax.numpy as jnp
from jax import lax

D = 8192
ROWS = 16
LAYERS = 2
PARITIES = 4
SPAN = 1024
N_DP = 128
N_PEER = 8


def draw_coef_num(key, part):
    key = jax.random.fold_in(key, 7)
    first, second = jax.random.split(key)
    sizes = jax.random.randint(first, (PARITIES, N_PEER), 1, 9)
    signs = 2 * jax.random.randint(second, (PARITIES, N_PEER), 0, 2) - 1
    return (sizes * signs).astype(jnp.int32)


def level_of(rng, shape, pieces, least, largest):
    factor_of = 1.0
    for axis_at, parts in pieces:
        heights = jax.random.uniform(jax.random.fold_in(jax.random.fold_in(rng, 6), axis_at), (parts,), jnp.float32, least / len(pieces), largest / len(pieces))
        factor_of = factor_of * jnp.repeat(jnp.exp(heights), shape[axis_at] // parts).reshape((-1,) + (1,) * (len(shape) - 1 - axis_at))
    return factor_of


def normal_values(key, extent, spread, bound, shards=(), dtype=jnp.bfloat16):
    array = spread * jax.random.normal(key, extent, jnp.float32)
    if shards:
        array = array * level_of(key, extent, shards, -0.22, 0.18)
    return jnp.clip(array, -bound, bound).astype(dtype)


def setup_inputs(seed: int = 0) -> dict:
    keys = jax.random.split(jax.random.key(seed), 9)
    grads = normal_values(keys[0], (N_DP, LAYERS, N_PEER * ROWS, D), 0.1, 0.796875, ((0, 128), (2, 8)))
    params = normal_values(keys[1], (LAYERS, N_PEER, N_DP * SPAN), 1.0, 6.0, ((1, 8), (2, 128)), jnp.float32)
    moment1 = normal_values(keys[2], (LAYERS, N_PEER, N_DP * SPAN), 0.3, 2.0, ((1, 8), (2, 128)), jnp.float32)
    moment2 = jnp.clip(jnp.exp(math.log(1.0) - 4.6051702 * jax.random.uniform(keys[3], (LAYERS, N_PEER, N_DP * SPAN), jnp.float32) ** level_of(keys[3], (LAYERS, N_PEER, N_DP * SPAN), ((1, 8), (2, 128)), -0.2, 0.2)), 0.01, 1.0)
    base_params = normal_values(keys[4], (LAYERS, N_PEER, N_DP * SPAN), 1.0, 6.0, ((1, 8), (2, 128)), jnp.float32)
    base_m1 = normal_values(keys[5], (LAYERS, N_PEER, N_DP * SPAN), 0.3, 2.0, ((1, 8), (2, 128)), jnp.float32)
    base_m2 = jnp.clip(jnp.exp(math.log(1.0) - 4.6051702 * jax.random.uniform(keys[6], (LAYERS, N_PEER, N_DP * SPAN), jnp.float32) ** level_of(keys[6], (LAYERS, N_PEER, N_DP * SPAN), ((1, 8), (2, 128)), -0.2, 0.2)), 0.01, 1.0)
    coef_num = draw_coef_num(jax.random.fold_in(keys[8], 71), 0)
    return dict(grads=grads, params=params, moment1=moment1, moment2=moment2, base_params=base_params, base_m1=base_m1, base_m2=base_m2, coef_num=coef_num)


def reference(grads, params, moment1, moment2, base_params, base_m1, base_m2, coef_num):

    def add_one(total, piece):
        return (total + piece.astype(jnp.float32), None)
    start = jnp.zeros(grads.shape[1:], jnp.float32)
    summed, unused = lax.scan(add_one, start, grads)
    g = summed.reshape(params.shape)
    new_m1 = 0.9 * moment1 + 0.1 * g
    new_m2 = 0.95 * moment2 + 0.05 * g * g
    fix_one = 1.0 - 0.9 ** 10
    fix_two = 1.0 - 0.95 ** 10
    new_params = params - 0.01 * (new_m1 / fix_one / (jnp.sqrt(new_m2 / fix_two) + 1e-08) + 0.1 * params)
    weights = new_params.astype(jnp.bfloat16).reshape(summed.shape)
    delta = jnp.stack([new_params - base_params, new_m1 - base_m1, new_m2 - base_m2], 0)
    coef = coef_num.astype(jnp.float32) / 8.0
    parity = jnp.einsum('pj,sljx->pslx', coef, delta, precision=lax.Precision.HIGHEST)
    return (new_params, new_m1, new_m2, weights, parity)
```

```python
import jax
import jax.numpy as jnp
from jax import lax
from jax.sharding import PartitionSpec as P

LANES = 128


def adamw(g, params, moment1, moment2):
    new_m1 = 0.9 * moment1 + 0.1 * g
    new_m2 = 0.95 * moment2 + 0.05 * g * g
    fix_one = 1.0 - 0.9**10
    fix_two = 1.0 - 0.95**10
    new_params = params - 0.01 * (
        new_m1 / fix_one / (jnp.sqrt(new_m2 / fix_two) + 1e-08) + 0.1 * params
    )
    return (new_params, new_m1, new_m2)


def body(grads, params, moment1, moment2, base_params, base_m1, base_m2, coef_num):
    _, layers, rows, width = grads.shape
    groups = lax.axis_size("dp")
    peers = lax.axis_size("peer")
    span = params.shape[2]
    per_row = width // span
    blocks = span // LANES
    tall = (layers * blocks, LANES)

    pieces = grads.reshape(layers, rows, per_row, blocks, LANES)
    pieces = pieces.transpose(1, 2, 0, 3, 4).reshape(groups, *tall)
    arrived = lax.all_to_all(pieces, "dp", 0, 0, tiled=True)
    g = jnp.sum(arrived.astype(jnp.float32), axis=0)

    new_params, new_m1, new_m2 = adamw(
        g, params.reshape(tall), moment1.reshape(tall), moment2.reshape(tall)
    )

    mine = new_params.astype(jnp.bfloat16)
    gathered = lax.all_to_all(
        jnp.broadcast_to(mine[None], (groups, *tall)), "dp", 0, 0, tiled=True
    )
    weights = gathered.reshape(rows, per_row, layers, blocks, LANES)
    weights = weights.transpose(2, 0, 1, 3, 4).reshape(layers, rows, width)

    delta = jnp.stack(
        [
            new_params - base_params.reshape(tall),
            new_m1 - base_m1.reshape(tall),
            new_m2 - base_m2.reshape(tall),
        ],
        0,
    ).reshape(3 * layers, blocks, LANES)
    delta = delta.reshape(3 * layers, peers, -1).transpose(1, 0, 2)
    deltas = lax.all_to_all(delta, "peer", 0, 0, tiled=True)
    coef = coef_num.astype(jnp.float32) / 8.0
    parity = jnp.sum(coef[:, :, None, None] * deltas[None], axis=1)
    parity = parity.reshape(coef.shape[0], 3, layers, span // peers)

    own = params.shape
    return (new_params.reshape(own), new_m1.reshape(own), new_m2.reshape(own), weights, parity)


def solution(mesh):
    state = P(None, "peer", "dp")
    return jax.shard_map(
        body,
        mesh=mesh,
        in_specs=(P("dp", None, "peer", None),) + (state,) * 6 + (P(),),
        out_specs=(
            state,
            state,
            state,
            P(None, "peer", None),
            P(None, None, None, ("dp", "peer")),
        ),
        check_vma=False,
    )
```

```python
import jax
import jax.numpy as jnp
from jax import lax
from jax.experimental import pallas as pl
from jax.experimental.pallas import tpu as pltpu
from jax.sharding import PartitionSpec as P

LANES = 128


def adamw(g, params, moment1, moment2):
    new_m1 = 0.9 * moment1 + 0.1 * g
    new_m2 = 0.95 * moment2 + 0.05 * g * g
    fix_one = 1.0 - 0.9**10
    fix_two = 1.0 - 0.95**10
    new_params = params - 0.01 * (
        new_m1 / fix_one / (jnp.sqrt(new_m2 / fix_two) + 1e-08) + 0.1 * params
    )
    return (new_params, new_m1, new_m2)


def update_kernel(
    arrived, params, moment1, moment2, base_params, base_m1, base_m2,
    new_params, new_m1, new_m2, spread, delta,
):
    layers = 2
    peers = delta.shape[0]
    g = jnp.sum(arrived[...].astype(jnp.float32), axis=0)
    p, m1, m2 = adamw(g, params[...], moment1[...], moment2[...])
    spread[...] = jnp.broadcast_to(p.astype(jnp.bfloat16)[None], spread.shape)
    new_params[...] = p
    new_m1[...] = m1
    new_m2[...] = m2
    changes = (p - base_params[...], m1 - base_m1[...], m2 - base_m2[...])
    for s, change in enumerate(changes):
        for l in range(layers):
            for j in range(peers):
                delta[j, s * layers + l, :] = change[l * peers + j, :]


def update(arrived, *state):
    groups = arrived.shape[0]
    tall = arrived.shape[1:]
    whole = pl.BlockSpec(memory_space=pltpu.VMEM)
    f32 = jax.ShapeDtypeStruct(tall, jnp.float32)
    return pl.pallas_call(
        update_kernel,
        out_shape=(
            f32,
            f32,
            f32,
            jax.ShapeDtypeStruct((groups, *tall), jnp.bfloat16),
            jax.ShapeDtypeStruct((8, 6, LANES), jnp.float32),
        ),
        in_specs=[whole] * 7,
        out_specs=(whole,) * 5,
        compiler_params=pltpu.CompilerParams(vmem_limit_bytes=8 * 2**20),
        name="update",
    )(arrived, *state)


def code_group(delta, coef_num):
    peers = delta.shape[0]
    me = lax.axis_index("peer")
    held = delta[:, None]
    source = [0]
    step = peers // 2
    while step >= 1:
        high = jnp.bitwise_and(me, step) != 0
        low_half, high_half = held[:step], held[step:]
        keep = jnp.where(high, high_half, low_half)
        send = jnp.where(high, low_half, high_half)
        got = lax.ppermute(send, "peer", [(i, i ^ step) for i in range(peers)])
        held = jnp.concatenate([keep, got], axis=1)
        source = source + [at ^ step for at in source]
        step //= 2
    order = jnp.bitwise_xor(me, jnp.array(source, jnp.int32))
    coef = coef_num.astype(jnp.float32) / 8.0
    picker = (jnp.arange(peers, dtype=jnp.int32)[None, :] == order[:, None]).astype(jnp.float32)
    column = jnp.sum(coef[:, None, :] * picker[None], axis=2)
    return jnp.sum(column[:, :, None, None] * held[0][None], axis=1)


def body(grads, params, moment1, moment2, base_params, base_m1, base_m2, coef_num):
    _, layers, rows, width = grads.shape
    groups = lax.axis_size("dp")
    peers = lax.axis_size("peer")
    own = params.shape
    span = own[2]
    per_row = width // span
    blocks = span // LANES
    tall = (layers * blocks, LANES)

    pieces = grads.reshape(layers, rows, per_row, blocks, LANES)
    pieces = pieces.transpose(1, 2, 0, 3, 4).reshape(groups, *tall)
    arrived = lax.all_to_all(pieces, "dp", 0, 0, tiled=True)

    state = (params, moment1, moment2, base_params, base_m1, base_m2)
    new_params, new_m1, new_m2, spread, delta = update(
        arrived, *(array.reshape(tall) for array in state)
    )

    gathered = lax.all_to_all(spread, "dp", 0, 0, tiled=True)
    weights = gathered.reshape(rows, per_row, layers, blocks, LANES)
    weights = weights.transpose(2, 0, 1, 3, 4).reshape(layers, rows, width)

    parity = code_group(delta, coef_num)
    parity = parity.reshape(parity.shape[0], 3, layers, span // peers)

    return (new_params.reshape(own), new_m1.reshape(own), new_m2.reshape(own), weights, parity)


def solution(mesh):
    state = P(None, "peer", "dp")
    return jax.shard_map(
        body,
        mesh=mesh,
        in_specs=(P("dp", None, "peer", None),) + (state,) * 6 + (P(),),
        out_specs=(
            state,
            state,
            state,
            P(None, "peer", None),
            P(None, None, None, ("dp", "peer")),
        ),
        check_vma=False,
    )
```

```python
import jax
import jax.numpy as jnp
from jax import lax
from jax.experimental import pallas as pl
from jax.experimental.pallas import tpu as pltpu
from jax.sharding import PartitionSpec as P

LANES = 128


def adamw(g, params, moment1, moment2):
    new_m1 = 0.9 * moment1 + 0.1 * g
    new_m2 = 0.95 * moment2 + 0.05 * g * g
    fix_one = 1.0 - 0.9**10
    fix_two = 1.0 - 0.95**10
    new_params = params - 0.01 * (
        new_m1 / fix_one / (jnp.sqrt(new_m2 / fix_two) + 1e-08) + 0.1 * params
    )
    return (new_params, new_m1, new_m2)


def ring(peer):
    return peer ^ ((peer & 4) >> 1)


def halving_order(peers):
    slots, step = [0], peers // 2
    while step >= 1:
        slots = slots + [at + step for at in slots]
        step //= 2
    return [slots[ring(j)] for j in range(peers)]


def update_kernel(
    arrived, params, moment1, moment2, base_params, base_m1, base_m2,
    new_params, new_m1, new_m2, spread, delta,
):
    layers = 2
    peers = delta.shape[0]
    g = jnp.sum(arrived[...].astype(jnp.float32), axis=0)
    p, m1, m2 = adamw(g, params[...], moment1[...], moment2[...])
    spread[...] = jnp.broadcast_to(p.astype(jnp.bfloat16)[None], spread.shape)
    new_params[...] = p
    new_m1[...] = m1
    new_m2[...] = m2
    slots = halving_order(peers)
    changes = (p - base_params[...], m1 - base_m1[...], m2 - base_m2[...])
    for s, change in enumerate(changes):
        for l in range(layers):
            for j in range(peers):
                delta[slots[j], s * layers + l, :] = change[l * peers + j, :]


def update(arrived, *state):
    groups = arrived.shape[0]
    tall = arrived.shape[1:]
    whole = pl.BlockSpec(memory_space=pltpu.VMEM)
    f32 = jax.ShapeDtypeStruct(tall, jnp.float32)
    return pl.pallas_call(
        update_kernel,
        out_shape=(
            f32,
            f32,
            f32,
            jax.ShapeDtypeStruct((groups, *tall), jnp.bfloat16),
            jax.ShapeDtypeStruct((8, 6, LANES), jnp.float32),
        ),
        in_specs=[whole] * 7,
        out_specs=(whole,) * 5,
        compiler_params=pltpu.CompilerParams(vmem_limit_bytes=8 * 2**20),
        name="update",
    )(arrived, *state)


def code_group(delta, coef_num):
    peers = delta.shape[0]
    delta, me = lax.optimization_barrier((delta, lax.axis_index("peer")))
    held = delta[:, None]
    label = ring(me)
    step = 1
    while step < peers:
        high = jnp.bitwise_and(label, step) != 0
        low_half, high_half = jnp.split(held, 2, axis=0)
        keep = jnp.where(high, high_half, low_half)
        send = jnp.where(high, low_half, high_half)
        got = lax.ppermute(send, "peer", [(i, i ^ ring(step)) for i in range(peers)])
        held = jnp.concatenate([keep, got], axis=1)
        step *= 2
    order = ring(jnp.bitwise_xor(label, jnp.arange(peers, dtype=jnp.int32)))
    coef = coef_num.astype(jnp.float32) / 8.0
    picker = (jnp.arange(peers, dtype=jnp.int32)[None, :] == order[:, None]).astype(jnp.float32)
    column = jnp.sum(coef[:, None, :] * picker[None], axis=2)
    return jnp.sum(column[:, :, None, None] * held[0][None], axis=1)


def body(grads, params, moment1, moment2, base_params, base_m1, base_m2, coef_num):
    _, layers, rows, width = grads.shape
    groups = lax.axis_size("dp")
    peers = lax.axis_size("peer")
    own = params.shape
    span = own[2]
    per_row = width // span
    blocks = span // LANES
    tall = (layers * blocks, LANES)

    pieces = grads.reshape(layers, rows, per_row, blocks, LANES)
    pieces = pieces.transpose(1, 2, 0, 3, 4).reshape(groups, *tall)
    arrived = lax.all_to_all(pieces, "dp", 0, 0, tiled=True)

    state = (params, moment1, moment2, base_params, base_m1, base_m2)
    new_params, new_m1, new_m2, spread, delta = update(
        arrived, *(array.reshape(tall) for array in state)
    )

    gathered = lax.all_to_all(spread, "dp", 0, 0, tiled=True)
    weights = gathered.reshape(rows, per_row, layers, blocks, LANES)
    weights = weights.transpose(2, 0, 1, 3, 4).reshape(layers, rows, width)

    delta, coef_num = lax.optimization_barrier((delta, coef_num))
    parity = code_group(delta, coef_num)
    parity = parity.reshape(parity.shape[0], 3, layers, span // peers)

    return (new_params.reshape(own), new_m1.reshape(own), new_m2.reshape(own), weights, parity)


def solution(mesh):
    state = P(None, "peer", "dp")
    return jax.shard_map(
        body,
        mesh=mesh,
        in_specs=(P("dp", None, "peer", None),) + (state,) * 6 + (P(),),
        out_specs=(
            state,
            state,
            state,
            P(None, "peer", None),
            P(None, None, None, ("dp", "peer")),
        ),
        check_vma=False,
    )
```

```python
import jax
import jax.numpy as jnp
from jax import lax
from jax.experimental import pallas as pl
from jax.experimental.pallas import tpu as pltpu
from jax.sharding import PartitionSpec as P

LANES = 128


def adamw(g, params, moment1, moment2):
    new_m1 = 0.9 * moment1 + 0.1 * g
    new_m2 = 0.95 * moment2 + 0.05 * g * g
    fix_one = 1.0 - 0.9**10
    fix_two = 1.0 - 0.95**10
    new_params = params - 0.01 * (
        new_m1 / fix_one / (jnp.sqrt(new_m2 / fix_two) + 1e-08) + 0.1 * params
    )
    return (new_params, new_m1, new_m2)


def ring(peer):
    return peer ^ ((peer & 4) >> 1)


def halving_order(peers):
    slots, step = [0], peers // 2
    while step >= 1:
        slots = slots + [at + step for at in slots]
        step //= 2
    return [slots[ring(j)] for j in range(peers)]


def place_kernel(gathered, weights, wide, ready, departures):
    layers, rows, width = weights.shape
    tall = gathered.shape[1]
    per_row = gathered.shape[0] // rows
    span = width // per_row
    blocks = span // LANES
    stores = []
    for c in range(per_row):
        for r in range(rows):
            wide[c, r * tall : (r + 1) * tall, :] = gathered[r * per_row + c].astype(jnp.float32)
        for l in range(layers):
            for k in range(blocks):
                tile = wide[c, pl.ds(l * blocks + k, rows, stride=tall), :]
                ready[c, l, :, k * LANES : (k + 1) * LANES] = tile.astype(jnp.bfloat16)
        stores.append(
            pltpu.make_async_copy(
                ready.at[c], weights.at[:, :, pl.ds(c * span, span)], departures.at[c]
            )
        )
        stores[-1].start()
    for copy in stores:
        copy.wait()


def place(gathered, layers, rows, width):
    per_row = gathered.shape[0] // rows
    tall = gathered.shape[1]
    return pl.pallas_call(
        place_kernel,
        out_shape=jax.ShapeDtypeStruct((layers, rows, width), gathered.dtype),
        in_specs=[pl.BlockSpec(memory_space=pltpu.VMEM)],
        out_specs=pl.BlockSpec(memory_space=pltpu.HBM),
        scratch_shapes=[
            pltpu.VMEM((per_row, rows * tall, LANES), jnp.float32),
            pltpu.VMEM((per_row, layers, rows, width // per_row), gathered.dtype),
            pltpu.SemaphoreType.DMA((per_row,)),
        ],
        compiler_params=pltpu.CompilerParams(vmem_limit_bytes=8 * 2**20),
        name="place",
    )(gathered)


def update_kernel(arrived, *refs):
    state, (new_params, new_m1, new_m2, spread, delta, held, arrivals) = refs[:6], refs[6:]
    copies = [
        pltpu.make_async_copy(ref, held.at[at], arrivals.at[at]) for at, ref in enumerate(state)
    ]
    for copy in copies:
        copy.start()
    peers = delta.shape[0]
    layers = delta.shape[1] // 3
    g = jnp.sum(arrived[...].astype(jnp.float32), axis=0)
    for copy in copies:
        copy.wait()
    p, m1, m2 = adamw(g, held[0], held[1], held[2])
    spread[...] = jnp.broadcast_to(p.astype(jnp.bfloat16)[None], spread.shape)
    new_params[...] = p
    new_m1[...] = m1
    new_m2[...] = m2
    slots = halving_order(peers)
    changes = (p - held[3], m1 - held[4], m2 - held[5])
    for s, change in enumerate(changes):
        for l in range(layers):
            for j in range(peers):
                delta[slots[j], s * layers + l, :] = change[l * peers + j, :]


def update(arrived, peers, *state):
    groups, *tall = arrived.shape
    layers = tall[0] // peers
    whole = pl.BlockSpec(memory_space=pltpu.VMEM)
    f32 = jax.ShapeDtypeStruct(tuple(tall), jnp.float32)
    return pl.pallas_call(
        update_kernel,
        out_shape=(
            f32,
            f32,
            f32,
            jax.ShapeDtypeStruct(arrived.shape, jnp.bfloat16),
            jax.ShapeDtypeStruct((peers, 3 * layers, LANES), jnp.float32),
        ),
        in_specs=[whole] + [pl.BlockSpec(memory_space=pltpu.HBM)] * 6,
        out_specs=(whole,) * 5,
        scratch_shapes=[pltpu.VMEM((6, *tall), jnp.float32), pltpu.SemaphoreType.DMA((6,))],
        compiler_params=pltpu.CompilerParams(vmem_limit_bytes=8 * 2**20),
        name="update",
    )(arrived, *state)


def code_group(delta, coef_num, me):
    peers = delta.shape[0]
    held = delta[:, None]
    label = ring(me)
    step = 1
    while step < peers:
        high = jnp.bitwise_and(label, step) != 0
        low_half, high_half = jnp.split(held, 2, axis=0)
        keep = jnp.where(high, high_half, low_half)
        send = jnp.where(high, low_half, high_half)
        got = lax.ppermute(send, "peer", [(i, i ^ ring(step)) for i in range(peers)])
        held = jnp.concatenate([keep, got], axis=1)
        step *= 2
    order = ring(jnp.bitwise_xor(label, jnp.arange(peers, dtype=jnp.int32)))
    coef = coef_num.astype(jnp.float32) / 8.0
    picker = (jnp.arange(peers, dtype=jnp.int32)[None, :] == order[:, None]).astype(jnp.float32)
    column = jnp.sum(coef[:, None, :] * picker[None], axis=2)
    return jnp.sum(column[:, :, None, None] * held[0][None], axis=1)


def body(grads, params, moment1, moment2, base_params, base_m1, base_m2, coef_num):
    _, layers, rows, width = grads.shape
    groups = lax.axis_size("dp")
    peers = lax.axis_size("peer")
    own = params.shape
    span = own[2]
    per_row = width // span
    blocks = span // LANES
    tall = (layers * blocks, LANES)

    grads, me = lax.optimization_barrier((grads, lax.axis_index("peer")))
    pieces = grads.reshape(layers, rows, per_row, blocks, LANES)
    pieces = pieces.transpose(1, 2, 0, 3, 4).reshape(groups, *tall)
    arrived = lax.all_to_all(pieces, "dp", 0, 0, tiled=True)

    state = (params, moment1, moment2, base_params, base_m1, base_m2)
    new_params, new_m1, new_m2, spread, delta = update(
        arrived, peers, *(array.reshape(tall) for array in state)
    )

    gathered = lax.all_to_all(spread, "dp", 0, 0, tiled=True)
    weights = place(gathered, layers, rows, width)

    delta, coef_num, me = lax.optimization_barrier((delta, coef_num, me))
    parity = code_group(delta, coef_num, me)
    parity = parity.reshape(parity.shape[0], 3, layers, span // peers)

    return (new_params.reshape(own), new_m1.reshape(own), new_m2.reshape(own), weights, parity)


def solution(mesh):
    state = P(None, "peer", "dp")
    return jax.shard_map(
        body,
        mesh=mesh,
        in_specs=(P("dp", None, "peer", None),) + (state,) * 6 + (P(),),
        out_specs=(
            state,
            state,
            state,
            P(None, "peer", None),
            P(None, None, None, ("dp", "peer")),
        ),
        check_vma=False,
    )
```

```python
import jax
import jax.numpy as jnp
from jax import lax
from jax.experimental import pallas as pl
from jax.experimental.pallas import tpu as pltpu
from jax.sharding import PartitionSpec as P

LANES = 128
FIRST = 112


def listed(groups):
    return [[(FIRST + i) % groups for i in range(groups)]]


def adamw(g, params, moment1, moment2):
    new_m1 = 0.9 * moment1 + 0.1 * g
    new_m2 = 0.95 * moment2 + 0.05 * g * g
    fix_one = 1.0 - 0.9**10
    fix_two = 1.0 - 0.95**10
    new_params = params - 0.01 * (
        new_m1 / fix_one / (jnp.sqrt(new_m2 / fix_two) + 1e-08) + 0.1 * params
    )
    return (new_params, new_m1, new_m2)


def ring(peer):
    return peer ^ ((peer & 4) >> 1)


def halving_order(peers):
    slots, step = [0], peers // 2
    while step >= 1:
        slots = slots + [at + step for at in slots]
        step //= 2
    return [slots[ring(j)] for j in range(peers)]


def place_kernel(gathered, weights, wide, ready, departures):
    layers, rows, width = weights.shape
    tall = gathered.shape[1]
    per_row = gathered.shape[0] // rows
    span = width // per_row
    blocks = span // LANES
    stores = []
    for c in range(per_row):
        for r in range(rows):
            wide[c, r * tall : (r + 1) * tall, :] = gathered[
                (r - FIRST // per_row) % rows * per_row + c
            ].astype(jnp.float32)
        for l in range(layers):
            for k in range(blocks):
                tile = wide[c, pl.ds(l * blocks + k, rows, stride=tall), :]
                ready[c, l, :, k * LANES : (k + 1) * LANES] = tile.astype(jnp.bfloat16)
        stores.append(
            pltpu.make_async_copy(
                ready.at[c], weights.at[:, :, pl.ds(c * span, span)], departures.at[c]
            )
        )
        stores[-1].start()
    for copy in stores:
        copy.wait()


def place(gathered, layers, rows, width):
    per_row = gathered.shape[0] // rows
    tall = gathered.shape[1]
    return pl.pallas_call(
        place_kernel,
        out_shape=jax.ShapeDtypeStruct((layers, rows, width), gathered.dtype),
        in_specs=[pl.BlockSpec(memory_space=pltpu.VMEM)],
        out_specs=pl.BlockSpec(memory_space=pltpu.HBM),
        scratch_shapes=[
            pltpu.VMEM((per_row, rows * tall, LANES), jnp.float32),
            pltpu.VMEM((per_row, layers, rows, width // per_row), gathered.dtype),
            pltpu.SemaphoreType.DMA((per_row,)),
        ],
        compiler_params=pltpu.CompilerParams(vmem_limit_bytes=8 * 2**20),
        name="place",
    )(gathered)


def update_kernel(arrived, *refs):
    state, (new_params, new_m1, new_m2, spread, delta, held, arrivals) = refs[:6], refs[6:]
    copies = [
        pltpu.make_async_copy(ref, held.at[at], arrivals.at[at]) for at, ref in enumerate(state)
    ]
    for copy in copies:
        copy.start()
    peers = delta.shape[0]
    layers = delta.shape[1] // 3
    g = jnp.sum(arrived[...].astype(jnp.float32), axis=0)
    for copy in copies:
        copy.wait()
    p, m1, m2 = adamw(g, held[0], held[1], held[2])
    spread[...] = jnp.broadcast_to(p.astype(jnp.bfloat16)[None], spread.shape)
    new_params[...] = p
    new_m1[...] = m1
    new_m2[...] = m2
    slots = halving_order(peers)
    changes = (p - held[3], m1 - held[4], m2 - held[5])
    for s, change in enumerate(changes):
        for l in range(layers):
            for j in range(peers):
                delta[slots[j], s * layers + l, :] = change[l * peers + j, :]


def update(arrived, peers, *state):
    groups, *tall = arrived.shape
    layers = tall[0] // peers
    whole = pl.BlockSpec(memory_space=pltpu.VMEM)
    f32 = jax.ShapeDtypeStruct(tuple(tall), jnp.float32)
    return pl.pallas_call(
        update_kernel,
        out_shape=(
            f32,
            f32,
            f32,
            jax.ShapeDtypeStruct(arrived.shape, jnp.bfloat16),
            jax.ShapeDtypeStruct((peers, 3 * layers, LANES), jnp.float32),
        ),
        in_specs=[whole] + [pl.BlockSpec(memory_space=pltpu.HBM)] * 6,
        out_specs=(whole,) * 5,
        scratch_shapes=[pltpu.VMEM((6, *tall), jnp.float32), pltpu.SemaphoreType.DMA((6,))],
        compiler_params=pltpu.CompilerParams(vmem_limit_bytes=8 * 2**20),
        name="update",
    )(arrived, *state)


def code_group(delta, coef_num, me):
    peers = delta.shape[0]
    held = delta[:, None]
    label = ring(me)
    step = 1
    while step < peers:
        high = jnp.bitwise_and(label, step) != 0
        low_half, high_half = jnp.split(held, 2, axis=0)
        keep = jnp.where(high, high_half, low_half)
        send = jnp.where(high, low_half, high_half)
        got = lax.ppermute(send, "peer", [(i, i ^ ring(step)) for i in range(peers)])
        held = jnp.concatenate([keep, got], axis=1)
        step *= 2
    order = ring(jnp.bitwise_xor(label, jnp.arange(peers, dtype=jnp.int32)))
    coef = coef_num.astype(jnp.float32) / 8.0
    picker = (jnp.arange(peers, dtype=jnp.int32)[None, :] == order[:, None]).astype(jnp.float32)
    column = jnp.sum(coef[:, None, :] * picker[None], axis=2)
    return jnp.sum(column[:, :, None, None] * held[0][None], axis=1)


def body(grads, params, moment1, moment2, base_params, base_m1, base_m2, coef_num):
    _, layers, rows, width = grads.shape
    groups = lax.axis_size("dp")
    peers = lax.axis_size("peer")
    own = params.shape
    span = own[2]
    per_row = width // span
    blocks = span // LANES
    tall = (layers * blocks, LANES)

    grads, me = lax.optimization_barrier((grads, lax.axis_index("peer")))
    pieces = grads.reshape(layers, rows, per_row, blocks, LANES)
    pieces = jnp.roll(pieces.transpose(1, 2, 0, 3, 4), -(FIRST // per_row), axis=0)
    pieces = pieces.reshape(groups, *tall)
    arrived = lax.all_to_all(pieces, "dp", 0, 0, tiled=True, axis_index_groups=listed(groups))

    state = (params, moment1, moment2, base_params, base_m1, base_m2)
    new_params, new_m1, new_m2, spread, delta = update(
        arrived, peers, *(array.reshape(tall) for array in state)
    )

    gathered = lax.all_to_all(
        spread, "dp", 0, 0, tiled=True, axis_index_groups=listed(groups)
    )
    weights = place(gathered, layers, rows, width)

    delta, coef_num, me = lax.optimization_barrier((delta, coef_num, me))
    parity = code_group(delta, coef_num, me)
    parity = parity.reshape(parity.shape[0], 3, layers, span // peers)

    return (new_params.reshape(own), new_m1.reshape(own), new_m2.reshape(own), weights, parity)


def solution(mesh):
    state = P(None, "peer", "dp")
    return jax.shard_map(
        body,
        mesh=mesh,
        in_specs=(P("dp", None, "peer", None),) + (state,) * 6 + (P(),),
        out_specs=(
            state,
            state,
            state,
            P(None, "peer", None),
            P(None, None, None, ("dp", "peer")),
        ),
        check_vma=False,
    )
```

```python
import jax
import jax.numpy as jnp
from jax import lax
from jax.experimental import pallas as pl
from jax.experimental.pallas import tpu as pltpu
from jax.sharding import PartitionSpec as P

LANES = 128
FIRST = 112


def listed(groups):
    return [[(FIRST + i) % groups for i in range(groups)]]


def adamw(g, params, moment1, moment2):
    new_m1 = 0.9 * moment1 + 0.1 * g
    new_m2 = 0.95 * moment2 + 0.05 * g * g
    fix_one = 1.0 - 0.9**10
    fix_two = 1.0 - 0.95**10
    new_params = params - 0.01 * (
        new_m1 / fix_one / (jnp.sqrt(new_m2 / fix_two) + 1e-08) + 0.1 * params
    )
    return (new_params, new_m1, new_m2)


def ring(peer):
    return peer ^ ((peer & 4) >> 1)


def halving_order(peers):
    slots, step = [0], peers // 2
    while step >= 1:
        slots = slots + [at + step for at in slots]
        step //= 2
    return [slots[ring(j)] for j in range(peers)]


def place_kernel(gathered, weights, wide, ready, departures):
    layers, rows, width = weights.shape
    tall = gathered.shape[1]
    per_row = gathered.shape[0] // rows
    span = width // per_row
    blocks = span // LANES
    stores = []
    for c in range(per_row):
        for r in range(rows):
            wide[c, r * tall : (r + 1) * tall, :] = gathered[r * per_row + c].astype(jnp.float32)
        for l in range(layers):
            for k in range(blocks):
                tile = wide[c, pl.ds(l * blocks + k, rows, stride=tall), :]
                ready[c, l, :, k * LANES : (k + 1) * LANES] = tile.astype(jnp.bfloat16)
        stores.append(
            pltpu.make_async_copy(
                ready.at[c], weights.at[:, :, pl.ds(c * span, span)], departures.at[c]
            )
        )
        stores[-1].start()
    for copy in stores:
        copy.wait()


def place(gathered, layers, rows, width):
    per_row = gathered.shape[0] // rows
    tall = gathered.shape[1]
    return pl.pallas_call(
        place_kernel,
        out_shape=jax.ShapeDtypeStruct((layers, rows, width), gathered.dtype),
        in_specs=[pl.BlockSpec(memory_space=pltpu.VMEM)],
        out_specs=pl.BlockSpec(memory_space=pltpu.HBM),
        scratch_shapes=[
            pltpu.VMEM((per_row, rows * tall, LANES), jnp.float32),
            pltpu.VMEM((per_row, layers, rows, width // per_row), gathered.dtype),
            pltpu.SemaphoreType.DMA((per_row,)),
        ],
        compiler_params=pltpu.CompilerParams(vmem_limit_bytes=8 * 2**20),
        name="place",
    )(gathered)


def update_kernel(arrived, *refs):
    state, (new_params, new_m1, new_m2, spread, delta, held, arrivals) = refs[:6], refs[6:]
    copies = [
        pltpu.make_async_copy(ref, held.at[at], arrivals.at[at]) for at, ref in enumerate(state)
    ]
    for copy in copies:
        copy.start()
    peers = delta.shape[0]
    layers = delta.shape[1] // 3
    g = jnp.sum(arrived[...].astype(jnp.float32), axis=0)
    for copy in copies:
        copy.wait()
    p, m1, m2 = adamw(g, held[0], held[1], held[2])
    spread[...] = jnp.broadcast_to(p.astype(jnp.bfloat16)[None], spread.shape)
    new_params[...] = p
    new_m1[...] = m1
    new_m2[...] = m2
    slots = halving_order(peers)
    changes = (p - held[3], m1 - held[4], m2 - held[5])
    for s, change in enumerate(changes):
        for l in range(layers):
            for j in range(peers):
                delta[slots[j], s * layers + l, :] = change[l * peers + j, :]


def update(arrived, peers, *state):
    groups, *tall = arrived.shape
    layers = tall[0] // peers
    whole = pl.BlockSpec(memory_space=pltpu.VMEM)
    f32 = jax.ShapeDtypeStruct(tuple(tall), jnp.float32)
    return pl.pallas_call(
        update_kernel,
        out_shape=(
            f32,
            f32,
            f32,
            jax.ShapeDtypeStruct(arrived.shape, jnp.bfloat16),
            jax.ShapeDtypeStruct((peers, 3 * layers, LANES), jnp.float32),
        ),
        in_specs=[whole] + [pl.BlockSpec(memory_space=pltpu.HBM)] * 6,
        out_specs=(whole,) * 5,
        scratch_shapes=[pltpu.VMEM((6, *tall), jnp.float32), pltpu.SemaphoreType.DMA((6,))],
        compiler_params=pltpu.CompilerParams(vmem_limit_bytes=8 * 2**20),
        name="update",
    )(arrived, *state)


def code_group(delta, coef_num, me):
    peers = delta.shape[0]
    held = delta[:, None]
    label = ring(me)
    step = 1
    while step < peers:
        high = jnp.bitwise_and(label, step) != 0
        low_half, high_half = jnp.split(held, 2, axis=0)
        keep = jnp.where(high, high_half, low_half)
        send = jnp.where(high, low_half, high_half)
        got = lax.ppermute(send, "peer", [(i, i ^ ring(step)) for i in range(peers)])
        held = jnp.concatenate([keep, got], axis=1)
        step *= 2
    order = ring(jnp.bitwise_xor(label, jnp.arange(peers, dtype=jnp.int32)))
    coef = coef_num.astype(jnp.float32) / 8.0
    picker = (jnp.arange(peers, dtype=jnp.int32)[None, :] == order[:, None]).astype(jnp.float32)
    column = jnp.sum(coef[:, None, :] * picker[None], axis=2)
    return jnp.sum(column[:, :, None, None] * held[0][None], axis=1)


def body(grads, params, moment1, moment2, base_params, base_m1, base_m2, coef_num):
    _, layers, rows, width = grads.shape
    groups = lax.axis_size("dp")
    peers = lax.axis_size("peer")
    own = params.shape
    span = own[2]
    per_row = width // span
    blocks = span // LANES
    tall = (layers * blocks, LANES)

    grads, me = lax.optimization_barrier((grads, lax.axis_index("peer")))
    pieces = grads.reshape(layers, rows, per_row, blocks, LANES)
    pieces = jnp.roll(pieces.transpose(1, 2, 0, 3, 4), -(FIRST // per_row), axis=0)
    pieces = pieces.reshape(groups, *tall)
    arrived = lax.all_to_all(pieces, "dp", 0, 0, tiled=True, axis_index_groups=listed(groups))

    state = (params, moment1, moment2, base_params, base_m1, base_m2)
    new_params, new_m1, new_m2, spread, delta = update(
        arrived, peers, *(array.reshape(tall) for array in state)
    )

    gathered = lax.all_to_all(spread, "dp", 0, 0, tiled=True)
    weights = place(gathered, layers, rows, width)

    delta, coef_num, me = lax.optimization_barrier((delta, coef_num, me))
    parity = code_group(delta, coef_num, me)
    parity = parity.reshape(parity.shape[0], 3, layers, span // peers)

    return (new_params.reshape(own), new_m1.reshape(own), new_m2.reshape(own), weights, parity)


def solution(mesh):
    state = P(None, "peer", "dp")
    return jax.shard_map(
        body,
        mesh=mesh,
        in_specs=(P("dp", None, "peer", None),) + (state,) * 6 + (P(),),
        out_specs=(
            state,
            state,
            state,
            P(None, "peer", None),
            P(None, None, None, ("dp", "peer")),
        ),
        check_vma=False,
    )
```
